32 devices in a mesh: groups: 2 (over y), grid: 4 (over z), head: 4 (over x, core).
Axes of the slice: x: 2, y: 2, z: 4, core: 2. Of those that a mesh axis runs over, the one named last changes fastest.
Arguments:
- queries: bfloat16 [64, 4096], P(('groups', 'grid', 'head')), parts along dimension 0, may hold values from -200 to 200
- cache_keys: bfloat16 [4, 8192, 512], P('groups', 'grid', 'head'), parts along dimension 0, may hold values from -6 to 6
- cache_values: bfloat16 [4, 8192, 512], P('groups', 'grid', 'head'), parts along dimension 0, may hold values from -96 to 96
- stretch_keys: bfloat16 [64, 512], P(('groups', 'grid', 'head')), parts along dimension 0, may hold values from -9 to 9
- stretch_values: bfloat16 [64, 512], P(('groups', 'grid', 'head')), parts along dimension 0, may hold values from -96 to 96
- cache_lengths: int32 [4], P('groups'), parts along dimension 0, may hold values from 1024 to 8192, as said below
Outputs:
- attended: bfloat16 [64, 4096], P(('groups', 'grid'), 'head'), parts along dimension 0
The draws below stay inside these ranges and needn't reach their ends.
There are 2 independent parts, one for each index of `groups`. The reference program is written for one: setup_inputs(seed, part) draws one part's arguments, and reference() takes and returns one part's arrays. A program takes and returns all parts, laid end to end along the dimension named above; each array names one. Nothing has to cross between parts.
Inputs may be any that keep to these rules, and one draw needn't show every extreme that they name: `cache_lengths`: in every group some request has cache length exactly 8192.
All inputs are finite; a program needn't handle non-finite values.
Results may differ from the reference program's by a relative error of at most 0.0085.
Values may be sent and summed in bfloat16 or wider, within the bound.
A program may use at most 64 MiB of HBM per device.

```python
import math
import jax
import jax.numpy as jnp
from jax import lax

HD = 128
GROUP = 8
REQS = 2
CR = 8
CACHE_DEV = 2048
KVH = 4
HQ = 32
STRETCH = 32
QR = 16
CACHE = 8192
N_GRID = 4


def drawn_cache(key):
    return jnp.clip(jax.random.normal(jax.random.fold_in(key, 11), (REQS, CACHE, KVH * HD), jnp.float32), -6.0, 6.0)


def draw_cache_keys(key, part):
    base = drawn_cache(key)
    return base.astype(jnp.bfloat16)


def draw_queries(key, part):
    values = jnp.clip(1.5 * jax.random.normal(jax.random.fold_in(key, 31), (STRETCH, HQ * HD), jnp.float32), -9.0, 9.0)
    return values.astype(jnp.bfloat16)


def draw_cache_lengths(key, part):
    first_key, second_key = jax.random.split(key)
    lengths = jax.random.randint(first_key, (REQS,), CACHE // 8, CACHE + 1)
    full_one = jax.random.randint(second_key, (), 0, REQS)
    return jnp.where(jnp.arange(REQS, dtype=jnp.int32) == full_one, CACHE, lengths).astype(jnp.int32)


def shard_levels(stream_key, extent, pieces, least, largest):
    def one(position, parts):
        heights = jax.random.uniform(jax.random.fold_in(jax.random.fold_in(stream_key, 6), position), (parts,), jnp.float32, least / len(pieces), largest / len(pieces))
        return jnp.repeat(jnp.exp(heights), extent[position] // parts).reshape((-1,) + (1,) * (len(extent) - position - 1))

    level = one(*pieces[0])
    for cut in pieces[1:]:
        level = level * one(*cut)
    return level


def noise(stream_key, shape, spread, bound, shards=(), kind=jnp.bfloat16):
    values = jax.random.normal(stream_key, shape, jnp.float32) * spread
    if len(shards) > 0:
        values = shard_levels(stream_key, shape, shards, -0.22, 0.18) * values
    return jnp.clip(values, min=-bound, max=bound).astype(kind)


def setup_inputs(seed: int = 0, part: int = 0) -> dict:
    key_list = jax.random.split(jax.random.key(seed), 7)
    part_keys = jax.random.split(jax.random.fold_in(key_list[6], part), 7)
    queries = draw_queries(jax.random.fold_in(jax.random.fold_in(key_list[6], part), 71), part)
    cache_keys = draw_cache_keys(jax.random.fold_in(jax.random.fold_in(key_list[6], part), 71), part)
    cache_values = noise(part_keys[2], (REQS, CACHE, KVH * HD), 16.0, 96.0, ((1, 4), (2, 4)))
    stretch_keys = noise(part_keys[3], (STRETCH, KVH * HD), 1.5, 9.0, ((0, 16),))
    stretch_values = noise(part_keys[4], (STRETCH, KVH * HD), 16.0, 96.0, ((0, 16),))
    cache_lengths = draw_cache_lengths(jax.random.fold_in(jax.random.fold_in(key_list[6], part), 71), part)
    return dict(queries=queries, cache_keys=cache_keys, cache_values=cache_values, stretch_keys=stretch_keys, stretch_values=stretch_values, cache_lengths=cache_lengths)


NEG = -1e+30

def block_partials(queries, keys, values, near_keys, near_values, cache_lengths, block):
    scale = 1.0 / math.sqrt(HD)
    key_pos = block * CACHE_DEV + jnp.arange(CACHE_DEV, dtype=jnp.int32)
    stretch_pos = block * CR + jnp.arange(CR, dtype=jnp.int32)
    near_k = near_keys.astype(jnp.float32).reshape(CR, KVH, HD)
    near_v = near_values.astype(jnp.float32).reshape(CR, KVH, HD)
    tops, totals, sums = ([], [], [])
    for request in range(REQS):
        query = queries[request * QR:(request + 1) * QR].astype(jnp.float32).reshape(QR, KVH, GROUP, HD)
        query_pos = request * QR + jnp.arange(QR, dtype=jnp.int32)
        near = (stretch_pos[None, :] // QR == request) & (stretch_pos[None, :] <= query_pos[:, None])
        near = near[:, None, None, :]
        near_scores = jnp.einsum('qhjd,chd->qhjc', query, near_k) * scale
        near_top = jnp.maximum(NEG, lax.optimization_barrier(jnp.max(jnp.where(near, near_scores, NEG), axis=3)))
        far_k = keys[request].astype(jnp.float32).reshape(CACHE_DEV, KVH, HD)
        far_v = values[request].astype(jnp.float32).reshape(CACHE_DEV, KVH, HD)
        far = (key_pos < cache_lengths[request])[None, None, None, :]
        far_scores = jnp.einsum('qhjd,khd->qhjk', query, far_k) * scale
        top = jnp.maximum(near_top, lax.optimization_barrier(jnp.max(jnp.where(far, far_scores, NEG), axis=3)))
        far_w = jnp.where(far, jnp.exp(far_scores - top[..., None]), 0.0).astype(jnp.bfloat16).astype(jnp.float32)
        near_w = jnp.where(near, jnp.exp(near_scores - top[..., None]), 0.0).astype(jnp.bfloat16).astype(jnp.float32)
        total = lax.optimization_barrier(jnp.sum(far_w, axis=3)) + lax.optimization_barrier(jnp.sum(near_w, axis=3))
        summed = jnp.einsum('qhjk,khd->qhjd', far_w, far_v) + jnp.einsum('qhjc,chd->qhjd', near_w, near_v)
        tops.append(top.reshape(QR, HQ))
        totals.append(total.reshape(QR, HQ))
        sums.append(summed.reshape(QR, HQ, HD))
    return (jnp.concatenate(tops, 0), jnp.concatenate(totals, 0), jnp.concatenate(sums, 0))

def reference(queries, cache_keys, cache_values, stretch_keys, stretch_values, cache_lengths):

    def advance(carry, block):
        run_top, run_total, run_sum = carry
        keys = lax.dynamic_slice_in_dim(cache_keys, block * CACHE_DEV, CACHE_DEV, 1)
        values = lax.dynamic_slice_in_dim(cache_values, block * CACHE_DEV, CACHE_DEV, 1)
        near_keys = lax.dynamic_slice_in_dim(stretch_keys, block * CR, CR, 0)
        near_values = lax.dynamic_slice_in_dim(stretch_values, block * CR, CR, 0)
        top, total, summed = block_partials(queries, keys, values, near_keys, near_values, cache_lengths, block)
        rounded = (summed / jnp.maximum(total, 1.0)[..., None]).astype(jnp.bfloat16)
        rounded = lax.optimization_barrier(rounded).astype(jnp.float32)
        new_top = jnp.maximum(run_top, top)
        keep = jnp.exp(run_top - new_top)
        gain = jnp.exp(top - new_top) * total
        return ((new_top, run_total * keep + gain, run_sum * keep[..., None] + rounded * gain[..., None]), None)
    start = (jnp.full((STRETCH, HQ), NEG, jnp.float32), jnp.zeros((STRETCH, HQ), jnp.float32), jnp.zeros((STRETCH, HQ, HD), jnp.float32))
    final, unused = lax.scan(advance, start, jnp.arange(N_GRID, dtype=jnp.int32))
    return (final[2] / final[1][..., None]).reshape(STRETCH, HQ * HD).astype(jnp.bfloat16)
```

```python
import functools
import math

import jax
import jax.numpy as jnp
from jax import lax
from jax.experimental import pallas as pl
from jax.experimental.pallas import tpu as pltpu
from jax.sharding import PartitionSpec as P

HD = 128
GROUP = 8
REQS = 2
PAD = 16
BLOCK_SRC = 8

MASKED = -1e30
FLOOR = -1e29
LOG2_SCALE = math.log2(math.e) / math.sqrt(HD)

MESH = pl.DeviceIdType.MESH
F32 = jnp.float32
BF16 = jnp.bfloat16


def repeat(start, stop, body):
    if stop - start <= 16:
        for i in range(start, stop):
            body(i)
    else:

        def step(i, carry):
            body(i)
            return carry

        lax.fori_loop(start, stop, step, 0)


def attend(query, keys, values, near_keys, near_values, bias, near_seen):
    contract = (((1,), (1,)), ((), ()))
    scores = lax.dot_general(query, keys, contract, preferred_element_type=F32) + bias
    near = lax.dot_general(query, near_keys, contract, preferred_element_type=F32)
    near = jnp.where(near_seen, near, MASKED)
    top = jnp.maximum(jnp.max(scores, axis=1, keepdims=True), jnp.max(near, axis=1, keepdims=True))
    top = jnp.maximum(top, FLOOR)
    weights = jnp.exp2((scores - top) * LOG2_SCALE)
    near_w = jnp.exp2((near - top) * LOG2_SCALE)
    total = jnp.sum(weights, axis=1, keepdims=True) + jnp.sum(near_w, axis=1, keepdims=True)
    summed = jnp.dot(weights.astype(BF16), values, preferred_element_type=F32)
    summed = summed + jnp.dot(near_w.astype(BF16), near_values, preferred_element_type=F32)
    return top, total, summed


def kernel(
    nz, nh,
    q_in, k_in, v_in, sk_in, sv_in, len_in,
    out_ref,
    q_own, sk_own, sv_own, lens, keys, values,
    q_pack, kv_pack, q_msg, kv_msg, q_all, kv_all,
    sum_msg, stat_msg, sum_all, stat_all, merged,
    load_sem, cache_sem, q_send, q_recv, kv_send, kv_recv, sum_send, sum_recv, stat_send, stat_recv,
):
    n = nz * nh
    z, h = lax.axis_index("grid"), lax.axis_index("head")
    me = z * nh + h
    local_rows = q_own.shape[0]
    msg_rows = local_rows * GROUP
    span = keys.shape[1]
    own_rows = local_rows * nh
    per_req = own_rows * nz // REQS
    owner_rows = own_rows * GROUP
    block_rows = BLOCK_SRC * msg_rows
    blocks = n // BLOCK_SRC
    owners = block_rows // owner_rows

    def peer(k):
        other = lax.rem(me + k, n)
        return other // nh, lax.rem(other, nh)

    barrier = pltpu.get_barrier_semaphore()

    def greet(k):
        oz, oh = peer(k)
        pl.semaphore_signal(barrier, inc=1, device_id={"grid": oz, "head": oh}, device_id_type=MESH)

    repeat(1, n, greet)

    loads = [
        pltpu.make_async_copy(q_in, q_own, load_sem.at[0]),
        pltpu.make_async_copy(sk_in, sk_own, load_sem.at[1]),
        pltpu.make_async_copy(sv_in, sv_own, load_sem.at[2]),
        pltpu.make_async_copy(len_in, lens, load_sem.at[3]),
    ]
    for load in loads:
        load.start()
    cache_loads = []
    for r in range(REQS):
        pair = (
            pltpu.make_async_copy(k_in.at[r], keys.at[r], cache_sem.at[2 * r]),
            pltpu.make_async_copy(v_in.at[r], values.at[r], cache_sem.at[2 * r + 1]),
        )
        for load in pair:
            load.start()
        cache_loads.append(pair)

    kv_pack[...] = jnp.zeros_like(kv_pack)
    kv_all[nh:] = jnp.zeros((kv_all.shape[0] - nh,) + kv_all.shape[1:], BF16)
    loads[0].wait()
    q32 = q_own[...].astype(F32)
    for oh in range(nh):
        for j in range(GROUP):
            column = (oh * GROUP + j) * HD
            q_pack[pl.ds(oh * msg_rows + j, local_rows, stride=GROUP), :] = q32[:, column : column + HD]
    q_msg[...] = q_pack[...].astype(BF16).reshape(q_msg.shape)
    loads[1].wait()
    loads[2].wait()
    for t, own in enumerate((sk_own, sv_own)):
        own32 = own[...].astype(F32)
        for oh in range(nh):
            kv_pack[pl.ds((oh * 2 + t) * PAD, local_rows), :] = own32[:, oh * HD : (oh + 1) * HD]
    kv_msg[...] = kv_pack[...].astype(BF16).reshape(kv_msg.shape)

    pl.semaphore_wait(barrier, n - 1)

    def send_q(k):
        oz, oh = peer(k)
        pltpu.make_async_remote_copy(
            src_ref=q_msg.at[oh], dst_ref=q_all.at[me], send_sem=q_send, recv_sem=q_recv.at[me // BLOCK_SRC],
            device_id={"grid": oz, "head": oh}, device_id_type=MESH,
        ).start()

    repeat(1, n, send_q)
    pltpu.make_async_copy(q_msg.at[h], q_all.at[me], q_recv.at[me // BLOCK_SRC]).start()
    for k in range(1, nh):
        oh = lax.rem(h + k, nh)
        pltpu.make_async_remote_copy(
            src_ref=kv_msg.at[oh], dst_ref=kv_all.at[h], send_sem=kv_send, recv_sem=kv_recv,
            device_id={"grid": z, "head": oh}, device_id_type=MESH,
        ).start()
    pltpu.make_async_copy(kv_msg.at[h], kv_all.at[h], kv_recv).start()

    loads[3].wait()
    unrolled = blocks <= 4
    if not unrolled:
        for pair in cache_loads:
            for load in pair:
                load.wait()
    landed = kv_all.at[pl.ds(0, nh)]
    pltpu.make_async_copy(landed, landed, kv_recv).wait()
    near_cols = kv_all.shape[0] * PAD
    near_keys = kv_all[:, 0].reshape(near_cols, HD)
    near_values = kv_all[:, 1].reshape(near_cols, HD)
    key_pos = z * span + lax.broadcasted_iota(jnp.int32, (1, span), 1)
    col = lax.broadcasted_iota(jnp.int32, (block_rows, near_cols), 1)
    row = lax.broadcasted_iota(jnp.int32, (block_rows, near_cols), 0)
    near_pos = z * own_rows + (col // PAD) * local_rows + col % PAD
    near_real = (col % PAD < local_rows) & (col < nh * PAD)
    owner_row = lax.broadcasted_iota(jnp.int32, (owner_rows, 128), 0)
    owner_lane = lax.broadcasted_iota(jnp.int32, (owner_rows, 128), 1)
    diagonal = owner_lane % owner_rows == owner_row

    def one_block(blk):
        first_row = blk * (block_rows // GROUP)
        request = first_row // per_req
        sources = pl.ds(blk * BLOCK_SRC, BLOCK_SRC)
        if unrolled and first_row % per_req == 0:
            for load in cache_loads[request]:
                load.wait()
        pltpu.make_async_copy(q_all.at[sources], q_all.at[sources], q_recv.at[blk]).wait()
        query = q_all[sources].reshape(block_rows, HD)
        bias = jnp.where(key_pos < lens[request], 0.0, MASKED)
        near_seen = near_real & (near_pos // per_req == request) & (near_pos <= first_row + row // GROUP)
        top, total, summed = attend(query, keys[request], values[request], near_keys, near_values, bias, near_seen)
        summed = summed.astype(BF16)
        for o in range(owners):
            owner = blk * owners + o
            part = slice(o * owner_rows, (o + 1) * owner_rows)
            sum_msg[owner] = summed[part]
            for t, stat in enumerate((top, total)):
                stat_msg[owner, t : t + 1, :] = jnp.sum(
                    jnp.where(diagonal, stat[part], 0.0), axis=0, keepdims=True
                )

            @pl.when(owner != z)
            def _():
                pltpu.make_async_remote_copy(
                    src_ref=stat_msg.at[owner], dst_ref=stat_all.at[z], send_sem=stat_send, recv_sem=stat_recv,
                    device_id={"grid": owner, "head": h}, device_id_type=MESH,
                ).start()
                pltpu.make_async_remote_copy(
                    src_ref=sum_msg.at[owner], dst_ref=sum_all.at[z], send_sem=sum_send, recv_sem=sum_recv,
                    device_id={"grid": owner, "head": h}, device_id_type=MESH,
                ).start()

            @pl.when(owner == z)
            def _():
                pltpu.make_async_copy(stat_msg.at[owner], stat_all.at[z], stat_recv).start()
                pltpu.make_async_copy(sum_msg.at[owner], sum_all.at[z], sum_recv).start()

    if unrolled:
        for blk in range(blocks):
            one_block(blk)
    else:
        repeat(0, blocks, one_block)

    pltpu.make_async_copy(stat_all, stat_all, stat_recv).wait()
    tops = [stat_all[b, 0:1, :] for b in range(nz)]
    peak = functools.reduce(jnp.maximum, tops)
    shares = [jnp.exp2((top - peak) * LOG2_SCALE) for top in tops]
    total = sum(share * stat_all[b, 1:2, :] for b, share in enumerate(shares))
    shares = [share / total for share in shares]
    per_tile = 128 // owner_rows
    pltpu.make_async_copy(sum_all, sum_all, sum_recv).wait()
    acc = jnp.zeros((owner_rows, HD), F32)
    for b in range(0, nz, per_tile):
        share = shares[b]
        for o in range(1, per_tile):
            share = jnp.where(owner_lane >= o * owner_rows, shares[b + o], share)
        mix = jnp.where(diagonal, share, 0.0)
        high = mix.astype(BF16)
        low = (mix - high.astype(F32)).astype(BF16)
        sums = sum_all[pl.ds(b, per_tile)].reshape(per_tile * owner_rows, HD)
        acc = acc + jnp.dot(high, sums, preferred_element_type=F32)
        acc = acc + jnp.dot(low, sums, preferred_element_type=F32)
    merged[...] = acc
    for j in range(GROUP):
        out_ref[:, j * HD : (j + 1) * HD] = merged[pl.ds(j, own_rows, stride=GROUP), :].astype(BF16)

    sent = q_all.at[pl.ds(0, n - 1)]
    pltpu.make_async_copy(sent, sent, q_send).wait()
    sent = kv_all.at[pl.ds(0, nh - 1)]
    pltpu.make_async_copy(sent, sent, kv_send).wait()
    sent = stat_all.at[pl.ds(0, nz - 1)]
    pltpu.make_async_copy(sent, sent, stat_send).wait()
    sent = sum_all.at[pl.ds(0, nz - 1)]
    pltpu.make_async_copy(sent, sent, sum_send).wait()


def shards(queries, cache_keys, cache_values, stretch_keys, stretch_values, cache_lengths):
    nz, nh = lax.axis_size("grid"), lax.axis_size("head")
    n = nz * nh
    local_rows = queries.shape[0]
    msg_rows = local_rows * GROUP
    owner_rows = local_rows * nh * GROUP
    slots = -(-nh * PAD // 128) * 128 // PAD
    any_spec = pl.BlockSpec(memory_space=pl.ANY)
    vmem_spec = pl.BlockSpec(memory_space=pltpu.VMEM)
    dma = pltpu.SemaphoreType.DMA
    return pl.pallas_call(
        functools.partial(kernel, nz, nh),
        out_shape=jax.ShapeDtypeStruct((local_rows * nh, GROUP * HD), BF16),
        in_specs=[any_spec] * 6,
        out_specs=vmem_spec,
        scratch_shapes=[
            pltpu.VMEM(queries.shape, BF16),
            pltpu.VMEM(stretch_keys.shape, BF16),
            pltpu.VMEM(stretch_values.shape, BF16),
            pltpu.SMEM(cache_lengths.shape, jnp.int32),
            pltpu.VMEM(cache_keys.shape, BF16),
            pltpu.VMEM(cache_values.shape, BF16),
            pltpu.VMEM((nh * msg_rows, HD), F32),
            pltpu.VMEM((nh * 2 * PAD, HD), F32),
            pltpu.VMEM((nh, msg_rows, HD), BF16),
            pltpu.VMEM((nh, 2, PAD, HD), BF16),
            pltpu.VMEM((n, msg_rows, HD), BF16),
            pltpu.VMEM((slots, 2, PAD, HD), BF16),
            pltpu.VMEM((nz, owner_rows, HD), BF16),
            pltpu.VMEM((nz, 2, 128), F32),
            pltpu.VMEM((nz, owner_rows, HD), BF16),
            pltpu.VMEM((nz, 2, 128), F32),
            pltpu.VMEM((owner_rows, HD), F32),
            dma((4,)),
            dma((2 * REQS,)),
            dma,
            dma((n // BLOCK_SRC,)),
            dma,
            dma,
            dma,
            dma,
            dma,
            dma,
        ],
        compiler_params=pltpu.CompilerParams(
            collective_id=0, has_side_effects=True, vmem_limit_bytes=48 * 1024 * 1024
        ),
    )(queries, cache_keys, cache_values, stretch_keys, stretch_values, cache_lengths)


def solution(mesh):
    in_specs = (
        P(("groups", "grid", "head"), None),
        P("groups", "grid", "head"),
        P("groups", "grid", "head"),
        P(("groups", "grid", "head"), None),
        P(("groups", "grid", "head"), None),
        P("groups"),
    )
    out_specs = P(("groups", "grid"), "head")
    return jax.shard_map(shards, mesh=mesh, in_specs=in_specs, out_specs=out_specs, check_vma=False)
```

```python
import functools
import math

import jax
import jax.numpy as jnp
from jax import lax
from jax.experimental import pallas as pl
from jax.experimental.pallas import tpu as pltpu
from jax.sharding import PartitionSpec as P

HD = 128
GROUP = 8
REQS = 2
NEAR = 128
BLOCK_SRC = 8

MASKED = -1e30
FLOOR = -1e29
LOG2_SCALE = math.log2(math.e) / math.sqrt(HD)

MESH = pl.DeviceIdType.MESH
F32 = jnp.float32
BF16 = jnp.bfloat16


def repeat(start, stop, body):
    if stop - start <= 16:
        for i in range(start, stop):
            body(i)
    else:

        def step(i, carry):
            body(i)
            return carry

        lax.fori_loop(start, stop, step, 0)


def attend(query, keys, values, near_keys, near_values, bias, near_seen):
    contract = (((1,), (1,)), ((), ()))
    scores = lax.dot_general(query, keys, contract, preferred_element_type=F32) + bias
    near = lax.dot_general(query, near_keys, contract, preferred_element_type=F32)
    near = jnp.where(near_seen, near, MASKED)
    top = jnp.maximum(jnp.max(scores, axis=1, keepdims=True), jnp.max(near, axis=1, keepdims=True))
    top = jnp.maximum(top, FLOOR)
    weights = jnp.exp2((scores - top) * LOG2_SCALE)
    near_w = jnp.exp2((near - top) * LOG2_SCALE)
    total = jnp.sum(weights, axis=1, keepdims=True) + jnp.sum(near_w, axis=1, keepdims=True)
    summed = jnp.dot(weights.astype(BF16), values, preferred_element_type=F32)
    summed = summed + jnp.dot(near_w.astype(BF16), near_values, preferred_element_type=F32)
    return top, total, summed


def kernel(
    nz, nh,
    q_in, k_in, v_in, sk_in, sv_in, len_in,
    out_ref,
    lens, keys, values, q_all, kv_all, near_pack,
    sum_msg, stat_msg, sum_all, stat_all,
    len_sem, cache_sem, q_send, q_recv, kv_send, kv_recv, sum_send, sum_recv, stat_send, stat_recv,
):
    n = nz * nh
    z, h = lax.axis_index("grid"), lax.axis_index("head")
    me = z * nh + h
    local_rows = sk_in.shape[1]
    msg_rows = local_rows * GROUP
    span = keys.shape[1]
    own_rows = local_rows * nh
    per_req = own_rows * nz // REQS
    owner_rows = own_rows * GROUP
    block_rows = BLOCK_SRC * msg_rows
    blocks = n // BLOCK_SRC
    owners = block_rows // owner_rows

    def peer(k):
        other = lax.rem(me + k, n)
        return other // nh, lax.rem(other, nh)

    barrier = pltpu.get_barrier_semaphore()

    def greet(k):
        oz, oh = peer(k)
        pl.semaphore_signal(barrier, inc=1, device_id={"grid": oz, "head": oh}, device_id_type=MESH)

    repeat(1, n, greet)

    len_load = pltpu.make_async_copy(len_in, lens, len_sem)
    len_load.start()
    cache_loads = []
    for r in range(REQS):
        pair = (
            pltpu.make_async_copy(k_in.at[r], keys.at[r], cache_sem.at[2 * r]),
            pltpu.make_async_copy(v_in.at[r], values.at[r], cache_sem.at[2 * r + 1]),
        )
        for load in pair:
            load.start()
        cache_loads.append(pair)

    near_pack[...] = jnp.zeros_like(near_pack)
    pl.semaphore_wait(barrier, n - 1)

    def send_q(k):
        oz, oh = peer(k)
        pltpu.make_async_remote_copy(
            src_ref=q_in.at[oh], dst_ref=q_all.at[me], send_sem=q_send, recv_sem=q_recv.at[me // BLOCK_SRC],
            device_id={"grid": oz, "head": oh}, device_id_type=MESH,
        ).start()

    repeat(1, n, send_q)
    pltpu.make_async_copy(q_in.at[h], q_all.at[me], q_recv.at[me // BLOCK_SRC]).start()
    for k in range(1, nh):
        oh = lax.rem(h + k, nh)
        for t, own in enumerate((sk_in, sv_in)):
            pltpu.make_async_remote_copy(
                src_ref=own.at[oh], dst_ref=kv_all.at[t, h], send_sem=kv_send, recv_sem=kv_recv,
                device_id={"grid": z, "head": oh}, device_id_type=MESH,
            ).start()
    for t, own in enumerate((sk_in, sv_in)):
        pltpu.make_async_copy(own.at[h], kv_all.at[t, h], kv_recv).start()

    len_load.wait()
    unrolled = blocks <= 4
    if not unrolled:
        for pair in cache_loads:
            for load in pair:
                load.wait()
    pltpu.make_async_copy(kv_all, kv_all, kv_recv).wait()
    for t in range(2):
        for oh in range(nh):
            near_pack[t, oh * local_rows : (oh + 1) * local_rows, :] = kv_all[t, oh].astype(F32)
    near_keys = near_pack[0].astype(BF16)
    near_values = near_pack[1].astype(BF16)
    key_pos = z * span + lax.broadcasted_iota(jnp.int32, (1, span), 1)
    col = lax.broadcasted_iota(jnp.int32, (block_rows, NEAR), 1)
    row = lax.broadcasted_iota(jnp.int32, (block_rows, NEAR), 0)
    near_pos = z * own_rows + col
    near_real = col < own_rows
    block_pos = row // msg_rows * local_rows + row % local_rows
    owner_row = lax.broadcasted_iota(jnp.int32, (owner_rows, 128), 0)
    owner_lane = lax.broadcasted_iota(jnp.int32, (owner_rows, 128), 1)
    diagonal = owner_lane % owner_rows == owner_row
    out_pos = owner_row % own_rows
    out_source = out_pos // local_rows * msg_rows + owner_row // own_rows * local_rows + out_pos % local_rows
    out_diagonal = owner_lane % owner_rows == out_source

    def one_block(blk):
        first_row = blk * (block_rows // GROUP)
        request = first_row // per_req
        sources = pl.ds(blk * BLOCK_SRC, BLOCK_SRC)
        if unrolled and first_row % per_req == 0:
            for load in cache_loads[request]:
                load.wait()
        pltpu.make_async_copy(q_all.at[sources], q_all.at[sources], q_recv.at[blk]).wait()
        query = q_all[sources].reshape(block_rows, HD)
        bias = jnp.where(key_pos < lens[request], 0.0, MASKED)
        near_seen = near_real & (near_pos // per_req == request) & (near_pos <= first_row + block_pos)
        top, total, summed = attend(query, keys[request], values[request], near_keys, near_values, bias, near_seen)
        summed = summed.astype(BF16)
        for o in range(owners):
            owner = blk * owners + o
            part = slice(o * owner_rows, (o + 1) * owner_rows)
            sum_msg[owner] = summed[part]
            for t, stat in enumerate((top, total)):
                stat_msg[owner, t : t + 1, :] = jnp.sum(
                    jnp.where(diagonal, stat[part], 0.0), axis=0, keepdims=True
                )

            @pl.when(owner != z)
            def _():
                pltpu.make_async_remote_copy(
                    src_ref=stat_msg.at[owner], dst_ref=stat_all.at[z], send_sem=stat_send, recv_sem=stat_recv,
                    device_id={"grid": owner, "head": h}, device_id_type=MESH,
                ).start()
                pltpu.make_async_remote_copy(
                    src_ref=sum_msg.at[owner], dst_ref=sum_all.at[z], send_sem=sum_send, recv_sem=sum_recv,
                    device_id={"grid": owner, "head": h}, device_id_type=MESH,
                ).start()

            @pl.when(owner == z)
            def _():
                pltpu.make_async_copy(stat_msg.at[owner], stat_all.at[z], stat_recv).start()
                pltpu.make_async_copy(sum_msg.at[owner], sum_all.at[z], sum_recv).start()

    if unrolled:
        for blk in range(blocks):
            one_block(blk)
    else:
        repeat(0, blocks, one_block)

    pltpu.make_async_copy(stat_all, stat_all, stat_recv).wait()
    tops = [stat_all[b, 0:1, :] for b in range(nz)]
    peak = functools.reduce(jnp.maximum, tops)
    shares = [jnp.exp2((top - peak) * LOG2_SCALE) for top in tops]
    total = sum(share * stat_all[b, 1:2, :] for b, share in enumerate(shares))
    shares = [share / total for share in shares]
    per_tile = 128 // owner_rows
    pltpu.make_async_copy(sum_all, sum_all, sum_recv).wait()
    acc = jnp.zeros((owner_rows, HD), F32)
    for b in range(0, nz, per_tile):
        share = shares[b]
        for o in range(1, per_tile):
            share = jnp.where(owner_lane >= o * owner_rows, shares[b + o], share)
        mix = jnp.where(out_diagonal, share, 0.0)
        high = mix.astype(BF16)
        low = (mix - high.astype(F32)).astype(BF16)
        sums = sum_all[pl.ds(b, per_tile)].reshape(per_tile * owner_rows, HD)
        acc = acc + jnp.dot(high, sums, preferred_element_type=F32)
        acc = acc + jnp.dot(low, sums, preferred_element_type=F32)
    for j in range(GROUP):
        out_ref[:, j * HD : (j + 1) * HD] = acc[j * own_rows : (j + 1) * own_rows].astype(BF16)

    sent = q_all.at[pl.ds(0, n - 1)]
    pltpu.make_async_copy(sent, sent, q_send).wait()
    sent = kv_all.at[:, pl.ds(0, nh - 1)]
    pltpu.make_async_copy(sent, sent, kv_send).wait()
    sent = stat_all.at[pl.ds(0, nz - 1)]
    pltpu.make_async_copy(sent, sent, stat_send).wait()
    sent = sum_all.at[pl.ds(0, nz - 1)]
    pltpu.make_async_copy(sent, sent, sum_send).wait()


def shards(queries, cache_keys, cache_values, stretch_keys, stretch_values, cache_lengths):
    nz, nh = lax.axis_size("grid"), lax.axis_size("head")
    n = nz * nh
    local_rows = queries.shape[0]
    msg_rows = local_rows * GROUP
    owner_rows = local_rows * nh * GROUP
    queries = queries.reshape(local_rows, nh, GROUP, HD).transpose(1, 2, 0, 3).reshape(nh, msg_rows, HD)
    stretch_keys = stretch_keys.reshape(local_rows, nh, HD).transpose(1, 0, 2)
    stretch_values = stretch_values.reshape(local_rows, nh, HD).transpose(1, 0, 2)
    any_spec = pl.BlockSpec(memory_space=pl.ANY)
    vmem_spec = pl.BlockSpec(memory_space=pltpu.VMEM)
    dma = pltpu.SemaphoreType.DMA
    return pl.pallas_call(
        functools.partial(kernel, nz, nh),
        out_shape=pltpu.VMEM((local_rows * nh, GROUP * HD), BF16),
        in_specs=[any_spec] * 6,
        out_specs=vmem_spec,
        scratch_shapes=[
            pltpu.SMEM(cache_lengths.shape, jnp.int32),
            pltpu.VMEM(cache_keys.shape, BF16),
            pltpu.VMEM(cache_values.shape, BF16),
            pltpu.VMEM((n, msg_rows, HD), BF16),
            pltpu.VMEM((2, nh, local_rows, HD), BF16),
            pltpu.VMEM((2, NEAR, HD), F32),
            pltpu.VMEM((nz, owner_rows, HD), BF16),
            pltpu.VMEM((nz, 2, 128), F32),
            pltpu.VMEM((nz, owner_rows, HD), BF16),
            pltpu.VMEM((nz, 2, 128), F32),
            dma,
            dma((2 * REQS,)),
            dma,
            dma((n // BLOCK_SRC,)),
            dma,
            dma,
            dma,
            dma,
            dma,
            dma,
        ],
        compiler_params=pltpu.CompilerParams(
            collective_id=0, has_side_effects=True, vmem_limit_bytes=63 * 1024 * 1024
        ),
    )(queries, cache_keys, cache_values, stretch_keys, stretch_values, cache_lengths)


def solution(mesh):
    in_specs = (
        P(("groups", "grid", "head"), None),
        P("groups", "grid", "head"),
        P("groups", "grid", "head"),
        P(("groups", "grid", "head"), None),
        P(("groups", "grid", "head"), None),
        P("groups"),
    )
    out_specs = P(("groups", "grid"), "head")
    return jax.shard_map(shards, mesh=mesh, in_specs=in_specs, out_specs=out_specs, check_vma=False)
```

```python
import functools
import math

import jax
import jax.numpy as jnp
from jax import lax
from jax.experimental import pallas as pl
from jax.experimental.pallas import tpu as pltpu
from jax.sharding import PartitionSpec as P

HD = 128
GROUP = 8
REQS = 2
NEAR = 128
BLOCK_SRC = 8

MASKED = -1e30
FLOOR = -1e29
LOG2_SCALE = math.log2(math.e) / math.sqrt(HD)

MESH = pl.DeviceIdType.MESH
F32 = jnp.float32
BF16 = jnp.bfloat16


def repeat(start, stop, body):
    if stop - start <= 16:
        for i in range(start, stop):
            body(i)
    else:

        def step(i, carry):
            body(i)
            return carry

        lax.fori_loop(start, stop, step, 0)


def attend(query, keys, values, near_keys, near_values, bias, near_seen):
    contract = (((1,), (1,)), ((), ()))
    scores = lax.dot_general(query, keys, contract, preferred_element_type=F32) + bias
    near = lax.dot_general(query, near_keys, contract, preferred_element_type=F32)
    near = jnp.where(near_seen, near, MASKED)
    top = jnp.maximum(jnp.max(scores, axis=1, keepdims=True), jnp.max(near, axis=1, keepdims=True))
    top = jnp.maximum(top, FLOOR)
    weights = jnp.exp2((scores - top) * LOG2_SCALE)
    near_w = jnp.exp2((near - top) * LOG2_SCALE)
    total = jnp.sum(weights, axis=1, keepdims=True) + jnp.sum(near_w, axis=1, keepdims=True)
    summed = jnp.dot(weights.astype(BF16), values, preferred_element_type=F32)
    summed = summed + jnp.dot(near_w.astype(BF16), near_values, preferred_element_type=F32)
    return top, total, summed


def kernel(
    nz, nh,
    q_in, k_in, v_in, sk_in, sv_in, len_in,
    out_ref,
    q_own, sk_own, sv_own, lens, keys, values, q_all, kv_all, near_pack,
    sum_msg, stat_msg, sum_all, stat_all,
    load_sem, cache_sem, q_send, q_recv, kv_send, kv_recv, sum_send, sum_recv, stat_send, stat_recv,
):
    n = nz * nh
    z, h = lax.axis_index("grid"), lax.axis_index("head")
    me = z * nh + h
    local_rows = sk_in.shape[1]
    msg_rows = local_rows * GROUP
    span = keys.shape[1]
    own_rows = local_rows * nh
    per_req = own_rows * nz // REQS
    owner_rows = own_rows * GROUP
    block_rows = BLOCK_SRC * msg_rows
    blocks = n // BLOCK_SRC
    owners = block_rows // owner_rows

    def wrapped(index, size):
        return jnp.where(index >= size, index - size, index)

    def peer(k):
        other = n - k
        other = jnp.where(other <= me, other - 1, other)
        return lax.div(other, nh), lax.rem(other, nh)

    barrier = pltpu.get_barrier_semaphore()

    def greet(k):
        oz, oh = peer(n - k)
        pl.semaphore_signal(barrier, inc=1, device_id={"grid": oz, "head": oh}, device_id_type=MESH)

    repeat(1, n, greet)

    loads = [
        pltpu.make_async_copy(source, own, load_sem.at[i])
        for i, (source, own) in enumerate(((q_in, q_own), (sk_in, sk_own), (sv_in, sv_own), (len_in, lens)))
    ]
    for load in loads:
        load.start()
    cache_loads = []
    for r in range(REQS):
        pair = (
            pltpu.make_async_copy(k_in.at[r], keys.at[r], cache_sem.at[2 * r]),
            pltpu.make_async_copy(v_in.at[r], values.at[r], cache_sem.at[2 * r + 1]),
        )
        for load in pair:
            load.start()
        cache_loads.append(pair)

    near_pack[...] = jnp.zeros_like(near_pack)
    for load in loads[:3]:
        load.wait()
    pl.semaphore_wait(barrier, n - 1)

    def send_q(k):
        oz, oh = peer(k)
        pltpu.make_async_remote_copy(
            src_ref=q_own.at[oh], dst_ref=q_all.at[me], send_sem=q_send, recv_sem=q_recv.at[me // BLOCK_SRC],
            device_id={"grid": oz, "head": oh}, device_id_type=MESH,
        ).start()

    repeat(1, n, send_q)
    pltpu.make_async_copy(q_own.at[h], q_all.at[me], q_recv.at[me // BLOCK_SRC]).start()
    for k in range(1, nh):
        oh = wrapped(h + k, nh)
        for t, own in enumerate((sk_own, sv_own)):
            pltpu.make_async_remote_copy(
                src_ref=own.at[oh], dst_ref=kv_all.at[t, h], send_sem=kv_send, recv_sem=kv_recv,
                device_id={"grid": z, "head": oh}, device_id_type=MESH,
            ).start()
    for t, own in enumerate((sk_own, sv_own)):
        pltpu.make_async_copy(own.at[h], kv_all.at[t, h], kv_recv).start()

    loads[3].wait()
    unrolled = blocks <= 4
    if not unrolled:
        for pair in cache_loads:
            for load in pair:
                load.wait()
    pltpu.make_async_copy(kv_all, kv_all, kv_recv).wait()
    for t in range(2):
        for oh in range(nh):
            near_pack[t, oh * local_rows : (oh + 1) * local_rows, :] = kv_all[t, oh].astype(F32)
    near_keys = near_pack[0].astype(BF16)
    near_values = near_pack[1].astype(BF16)
    key_pos = z * span + lax.broadcasted_iota(jnp.int32, (1, span), 1)
    col = lax.broadcasted_iota(jnp.int32, (block_rows, NEAR), 1)
    row = lax.broadcasted_iota(jnp.int32, (block_rows, NEAR), 0)
    near_pos = z * own_rows + col
    near_real = col < own_rows
    block_pos = row // msg_rows * local_rows + row % local_rows
    owner_row = lax.broadcasted_iota(jnp.int32, (owner_rows, 128), 0)
    owner_lane = lax.broadcasted_iota(jnp.int32, (owner_rows, 128), 1)
    diagonal = owner_lane % owner_rows == owner_row
    out_pos = owner_row % own_rows
    out_source = out_pos // local_rows * msg_rows + owner_row // own_rows * local_rows + out_pos % local_rows
    out_diagonal = owner_lane % owner_rows == out_source

    def masks(blk):
        first_row = blk * (block_rows // GROUP)
        request = first_row // per_req
        bias = jnp.where(key_pos < lens[request], 0.0, MASKED)
        near_seen = near_real & (near_pos // per_req == request) & (near_pos <= first_row + block_pos)
        return request, bias, near_seen

    ready = [masks(blk) for blk in range(blocks)] if unrolled else None

    def one_block(blk):
        request, bias, near_seen = ready[blk] if unrolled else masks(blk)
        first_row = blk * (block_rows // GROUP)
        sources = pl.ds(blk * BLOCK_SRC, BLOCK_SRC)
        if unrolled and first_row % per_req == 0:
            for load in cache_loads[request]:
                load.wait()
        pltpu.make_async_copy(q_all.at[sources], q_all.at[sources], q_recv.at[blk]).wait()
        query = q_all[sources].reshape(block_rows, HD)
        top, total, summed = attend(query, keys[request], values[request], near_keys, near_values, bias, near_seen)
        summed = summed.astype(BF16)
        for o in range(owners):
            owner = blk * owners + o
            part = slice(o * owner_rows, (o + 1) * owner_rows)
            sum_msg[owner] = summed[part]
            for t, stat in enumerate((top, total)):
                stat_msg[owner, t : t + 1, :] = jnp.sum(
                    jnp.where(diagonal, stat[part], 0.0), axis=0, keepdims=True
                )

            @pl.when(owner != z)
            def _():
                pltpu.make_async_remote_copy(
                    src_ref=stat_msg.at[owner], dst_ref=stat_all.at[z], send_sem=stat_send, recv_sem=stat_recv,
                    device_id={"grid": owner, "head": h}, device_id_type=MESH,
                ).start()
                pltpu.make_async_remote_copy(
                    src_ref=sum_msg.at[owner], dst_ref=sum_all.at[z], send_sem=sum_send, recv_sem=sum_recv,
                    device_id={"grid": owner, "head": h}, device_id_type=MESH,
                ).start()

            @pl.when(owner == z)
            def _():
                pltpu.make_async_copy(stat_msg.at[owner], stat_all.at[z], stat_recv).start()
                pltpu.make_async_copy(sum_msg.at[owner], sum_all.at[z], sum_recv).start()

    if unrolled:
        for blk in range(blocks):
            one_block(blk)
    else:
        repeat(0, blocks, one_block)

    pltpu.make_async_copy(stat_all, stat_all, stat_recv).wait()
    tops = [stat_all[b, 0:1, :] for b in range(nz)]
    peak = functools.reduce(jnp.maximum, tops)
    shares = [jnp.exp2((top - peak) * LOG2_SCALE) for top in tops]
    total = sum(share * stat_all[b, 1:2, :] for b, share in enumerate(shares))
    shares = [share / total for share in shares]
    per_tile = 128 // owner_rows
    pltpu.make_async_copy(sum_all, sum_all, sum_recv).wait()
    acc = jnp.zeros((owner_rows, HD), F32)
    for b in range(0, nz, per_tile):
        share = shares[b]
        for o in range(1, per_tile):
            share = jnp.where(owner_lane >= o * owner_rows, shares[b + o], share)
        mix = jnp.where(out_diagonal, share, 0.0)
        high = mix.astype(BF16)
        low = (mix - high.astype(F32)).astype(BF16)
        sums = sum_all[pl.ds(b, per_tile)].reshape(per_tile * owner_rows, HD)
        acc = acc + jnp.dot(high, sums, preferred_element_type=F32)
        acc = acc + jnp.dot(low, sums, preferred_element_type=F32)
    for j in range(GROUP):
        out_ref[:, j * HD : (j + 1) * HD] = acc[j * own_rows : (j + 1) * own_rows].astype(BF16)

    sent = q_all.at[pl.ds(0, n - 1)]
    pltpu.make_async_copy(sent, sent, q_send).wait()
    sent = kv_all.at[:, pl.ds(0, nh - 1)]
    pltpu.make_async_copy(sent, sent, kv_send).wait()
    sent = stat_all.at[pl.ds(0, nz - 1)]
    pltpu.make_async_copy(sent, sent, stat_send).wait()
    sent = sum_all.at[pl.ds(0, nz - 1)]
    pltpu.make_async_copy(sent, sent, sum_send).wait()


def shards(queries, cache_keys, cache_values, stretch_keys, stretch_values, cache_lengths):
    nz, nh = lax.axis_size("grid"), lax.axis_size("head")
    n = nz * nh
    local_rows = queries.shape[0]
    msg_rows = local_rows * GROUP
    owner_rows = local_rows * nh * GROUP
    queries = queries.reshape(local_rows, nh, GROUP, HD).transpose(1, 2, 0, 3).reshape(nh, msg_rows, HD)
    stretch_keys = stretch_keys.reshape(local_rows, nh, HD).transpose(1, 0, 2)
    stretch_values = stretch_values.reshape(local_rows, nh, HD).transpose(1, 0, 2)
    any_spec = pl.BlockSpec(memory_space=pl.ANY)
    vmem_spec = pl.BlockSpec(memory_space=pltpu.VMEM)
    dma = pltpu.SemaphoreType.DMA
    return pl.pallas_call(
        functools.partial(kernel, nz, nh),
        out_shape=pltpu.VMEM((local_rows * nh, GROUP * HD), BF16),
        in_specs=[any_spec] * 6,
        out_specs=vmem_spec,
        scratch_shapes=[
            pltpu.VMEM(queries.shape, BF16),
            pltpu.VMEM(stretch_keys.shape, BF16),
            pltpu.VMEM(stretch_values.shape, BF16),
            pltpu.SMEM(cache_lengths.shape, jnp.int32),
            pltpu.VMEM(cache_keys.shape, BF16),
            pltpu.VMEM(cache_values.shape, BF16),
            pltpu.VMEM((n, msg_rows, HD), BF16),
            pltpu.VMEM((2, nh, local_rows, HD), BF16),
            pltpu.VMEM((2, NEAR, HD), F32),
            pltpu.VMEM((nz, owner_rows, HD), BF16),
            pltpu.VMEM((nz, 2, 128), F32),
            pltpu.VMEM((nz, owner_rows, HD), BF16),
            pltpu.VMEM((nz, 2, 128), F32),
            dma((4,)),
            dma((2 * REQS,)),
            dma,
            dma((n // BLOCK_SRC,)),
            dma,
            dma,
            dma,
            dma,
            dma,
            dma,
        ],
        compiler_params=pltpu.CompilerParams(
            collective_id=0, has_side_effects=True, vmem_limit_bytes=63 * 1024 * 1024
        ),
    )(queries, cache_keys, cache_values, stretch_keys, stretch_values, cache_lengths)


def solution(mesh):
    in_specs = (
        P(("groups", "grid", "head"), None),
        P("groups", "grid", "head"),
        P("groups", "grid", "head"),
        P(("groups", "grid", "head"), None),
        P(("groups", "grid", "head"), None),
        P("groups"),
    )
    out_specs = P(("groups", "grid"), "head")
    return jax.shard_map(shards, mesh=mesh, in_specs=in_specs, out_specs=out_specs, check_vma=False)
```

```python
import functools
import math

import jax
import jax.numpy as jnp
from jax import lax
from jax.experimental import pallas as pl
from jax.experimental.pallas import tpu as pltpu
from jax.sharding import PartitionSpec as P

HD = 128
GROUP = 8
REQS = 2
NEAR = 128
CHUNK = 512
BLOCK_SRC = 8

MASKED = -1e30
FLOOR = -1e29
LOG2_SCALE = math.log2(math.e) / math.sqrt(HD)

MESH = pl.DeviceIdType.MESH
F32 = jnp.float32
BF16 = jnp.bfloat16


def repeat(start, stop, body):
    if stop - start <= 16:
        for i in range(start, stop):
            body(i)
    else:

        def step(i, carry):
            body(i)
            return carry

        lax.fori_loop(start, stop, step, 0)


def attend(query, keys, values, near_keys, near_values, bias, near_seen):
    contract = (((1,), (1,)), ((), ()))
    span = keys.shape[0]
    chunk = math.gcd(span, CHUNK)
    parts = [slice(c, c + chunk) for c in range(0, span, chunk)]
    near = lax.dot_general(query, near_keys, contract, preferred_element_type=F32)
    near = jnp.where(near_seen, near, MASKED)
    scores = [
        lax.dot_general(query, keys[part], contract, preferred_element_type=F32) + bias[:, part] for part in parts
    ]
    lanes = near
    for score in scores:
        for c in range(0, chunk, NEAR):
            lanes = jnp.maximum(lanes, score[:, c : c + NEAR])
    top = jnp.maximum(jnp.max(lanes, axis=1, keepdims=True), FLOOR)
    near_w = jnp.exp2((near - top) * LOG2_SCALE)
    lanes = near_w
    summed = jnp.dot(near_w.astype(BF16), near_values, preferred_element_type=F32)
    for part, score in zip(parts, scores):
        weights = jnp.exp2((score - top) * LOG2_SCALE)
        for c in range(0, chunk, NEAR):
            lanes = lanes + weights[:, c : c + NEAR]
        summed = summed + jnp.dot(weights.astype(BF16), values[part], preferred_element_type=F32)
    total = jnp.sum(lanes, axis=1, keepdims=True)
    return top, total, summed


def kernel(
    nz, nh,
    q_in, k_in, v_in, sk_in, sv_in, len_in,
    out_ref,
    q_own, sk_own, sv_own, lens, keys, values, q_all, kv_all, near_pack,
    sum_msg, stat_msg, sum_all, stat_all,
    load_sem, cache_sem, q_send, q_recv, kv_send, kv_recv, sum_send, sum_recv, stat_send, stat_recv,
):
    n = nz * nh
    z, h = lax.axis_index("grid"), lax.axis_index("head")
    me = z * nh + h
    local_rows = sk_in.shape[1]
    msg_rows = local_rows * GROUP
    span = keys.shape[1]
    own_rows = local_rows * nh
    per_req = own_rows * nz // REQS
    owner_rows = own_rows * GROUP
    block_rows = BLOCK_SRC * msg_rows
    blocks = n // BLOCK_SRC
    owners = block_rows // owner_rows

    def wrapped(index, size):
        return jnp.where(index >= size, index - size, index)

    def peer(k):
        other = n - k
        other = jnp.where(other <= me, other - 1, other)
        return lax.div(other, nh), lax.rem(other, nh)

    barrier = pltpu.get_barrier_semaphore()

    def greet(k):
        oz, oh = peer(n - k)
        pl.semaphore_signal(barrier, inc=1, device_id={"grid": oz, "head": oh}, device_id_type=MESH)

    repeat(1, n, greet)

    loads = [
        pltpu.make_async_copy(source, own, load_sem.at[i])
        for i, (source, own) in enumerate(((q_in, q_own), (sk_in, sk_own), (sv_in, sv_own), (len_in, lens)))
    ]
    for load in loads:
        load.start()
    cache_loads = []
    for r in range(REQS):
        pair = (
            pltpu.make_async_copy(k_in.at[r], keys.at[r], cache_sem.at[2 * r]),
            pltpu.make_async_copy(v_in.at[r], values.at[r], cache_sem.at[2 * r + 1]),
        )
        for load in pair:
            load.start()
        cache_loads.append(pair)

    near_pack[...] = jnp.zeros_like(near_pack)
    for load in loads[:3]:
        load.wait()
    pl.semaphore_wait(barrier, n - 1)

    def send_q(k):
        oz, oh = peer(k)
        pltpu.make_async_remote_copy(
            src_ref=q_own.at[oh], dst_ref=q_all.at[me], send_sem=q_send, recv_sem=q_recv.at[me // BLOCK_SRC],
            device_id={"grid": oz, "head": oh}, device_id_type=MESH,
        ).start()

    repeat(1, n, send_q)
    pltpu.make_async_copy(q_own.at[h], q_all.at[me], q_recv.at[me // BLOCK_SRC]).start()
    for k in range(1, nh):
        oh = wrapped(h + k, nh)
        for t, own in enumerate((sk_own, sv_own)):
            pltpu.make_async_remote_copy(
                src_ref=own.at[oh], dst_ref=kv_all.at[t, h], send_sem=kv_send, recv_sem=kv_recv,
                device_id={"grid": z, "head": oh}, device_id_type=MESH,
            ).start()
    for t, own in enumerate((sk_own, sv_own)):
        pltpu.make_async_copy(own.at[h], kv_all.at[t, h], kv_recv).start()

    loads[3].wait()
    unrolled = blocks <= 4
    if not unrolled:
        for pair in cache_loads:
            for load in pair:
                load.wait()
    pltpu.make_async_copy(kv_all, kv_all, kv_recv).wait()
    for t in range(2):
        for oh in range(nh):
            near_pack[t, oh * local_rows : (oh + 1) * local_rows, :] = kv_all[t, oh].astype(F32)
    near_keys = near_pack[0].astype(BF16)
    near_values = near_pack[1].astype(BF16)
    key_pos = z * span + lax.broadcasted_iota(jnp.int32, (1, span), 1)
    col = lax.broadcasted_iota(jnp.int32, (block_rows, NEAR), 1)
    row = lax.broadcasted_iota(jnp.int32, (block_rows, NEAR), 0)
    near_pos = z * own_rows + col
    near_real = col < own_rows
    block_pos = row // msg_rows * local_rows + row % local_rows
    owner_row = lax.broadcasted_iota(jnp.int32, (owner_rows, 128), 0)
    owner_lane = lax.broadcasted_iota(jnp.int32, (owner_rows, 128), 1)
    diagonal = owner_lane % owner_rows == owner_row
    out_pos = owner_row % own_rows
    out_source = out_pos // local_rows * msg_rows + owner_row // own_rows * local_rows + out_pos % local_rows
    out_diagonal = owner_lane % owner_rows == out_source

    def masks(blk):
        first_row = blk * (block_rows // GROUP)
        request = first_row // per_req
        bias = jnp.where(key_pos < lens[request], 0.0, MASKED)
        near_seen = near_real & (near_pos // per_req == request) & (near_pos <= first_row + block_pos)
        return request, bias, near_seen

    ready = [masks(blk) for blk in range(blocks)] if unrolled else None

    def one_block(blk):
        request, bias, near_seen = ready[blk] if unrolled else masks(blk)
        first_row = blk * (block_rows // GROUP)
        sources = pl.ds(blk * BLOCK_SRC, BLOCK_SRC)
        if unrolled and first_row % per_req == 0:
            for load in cache_loads[request]:
                load.wait()
        pltpu.make_async_copy(q_all.at[sources], q_all.at[sources], q_recv.at[blk]).wait()
        query = q_all[sources].reshape(block_rows, HD)
        top, total, summed = attend(query, keys[request], values[request], near_keys, near_values, bias, near_seen)
        summed = summed.astype(BF16)
        for o in range(owners):
            owner = blk * owners + o
            part = slice(o * owner_rows, (o + 1) * owner_rows)
            sum_msg[owner] = summed[part]
            for t, stat in enumerate((top, total)):
                stat_msg[owner, t : t + 1, :] = jnp.sum(
                    jnp.where(diagonal, stat[part], 0.0), axis=0, keepdims=True
                )

            @pl.when(owner != z)
            def _():
                pltpu.make_async_remote_copy(
                    src_ref=stat_msg.at[owner], dst_ref=stat_all.at[z], send_sem=stat_send, recv_sem=stat_recv,
                    device_id={"grid": owner, "head": h}, device_id_type=MESH,
                ).start()
                pltpu.make_async_remote_copy(
                    src_ref=sum_msg.at[owner], dst_ref=sum_all.at[z], send_sem=sum_send, recv_sem=sum_recv,
                    device_id={"grid": owner, "head": h}, device_id_type=MESH,
                ).start()

            @pl.when(owner == z)
            def _():
                pltpu.make_async_copy(stat_msg.at[owner], stat_all.at[z], stat_recv).start()
                pltpu.make_async_copy(sum_msg.at[owner], sum_all.at[z], sum_recv).start()

    if unrolled:
        for blk in range(blocks):
            one_block(blk)
    else:
        repeat(0, blocks, one_block)

    pltpu.make_async_copy(stat_all, stat_all, stat_recv).wait()
    tops = [stat_all[b, 0:1, :] for b in range(nz)]
    peak = functools.reduce(jnp.maximum, tops)
    shares = [jnp.exp2((top - peak) * LOG2_SCALE) for top in tops]
    total = sum(share * stat_all[b, 1:2, :] for b, share in enumerate(shares))
    shares = [share / total for share in shares]
    per_tile = 128 // owner_rows
    pltpu.make_async_copy(sum_all, sum_all, sum_recv).wait()
    acc = jnp.zeros((owner_rows, HD), F32)
    for b in range(0, nz, per_tile):
        share = shares[b]
        for o in range(1, per_tile):
            share = jnp.where(owner_lane >= o * owner_rows, shares[b + o], share)
        mix = jnp.where(out_diagonal, share, 0.0)
        high = mix.astype(BF16)
        low = (mix - high.astype(F32)).astype(BF16)
        sums = sum_all[pl.ds(b, per_tile)].reshape(per_tile * owner_rows, HD)
        acc = acc + jnp.dot(high, sums, preferred_element_type=F32)
        acc = acc + jnp.dot(low, sums, preferred_element_type=F32)
    for j in range(GROUP):
        out_ref[:, j * HD : (j + 1) * HD] = acc[j * own_rows : (j + 1) * own_rows].astype(BF16)

    sent = q_all.at[pl.ds(0, n - 1)]
    pltpu.make_async_copy(sent, sent, q_send).wait()
    sent = kv_all.at[:, pl.ds(0, nh - 1)]
    pltpu.make_async_copy(sent, sent, kv_send).wait()
    sent = stat_all.at[pl.ds(0, nz - 1)]
    pltpu.make_async_copy(sent, sent, stat_send).wait()
    sent = sum_all.at[pl.ds(0, nz - 1)]
    pltpu.make_async_copy(sent, sent, sum_send).wait()


def shards(queries, cache_keys, cache_values, stretch_keys, stretch_values, cache_lengths):
    nz, nh = lax.axis_size("grid"), lax.axis_size("head")
    n = nz * nh
    local_rows = queries.shape[0]
    msg_rows = local_rows * GROUP
    owner_rows = local_rows * nh * GROUP
    queries = queries.reshape(local_rows, nh, GROUP, HD).transpose(1, 2, 0, 3).reshape(nh, msg_rows, HD)
    stretch_keys = stretch_keys.reshape(local_rows, nh, HD).transpose(1, 0, 2)
    stretch_values = stretch_values.reshape(local_rows, nh, HD).transpose(1, 0, 2)
    any_spec = pl.BlockSpec(memory_space=pl.ANY)
    vmem_spec = pl.BlockSpec(memory_space=pltpu.VMEM)
    dma = pltpu.SemaphoreType.DMA
    return pl.pallas_call(
        functools.partial(kernel, nz, nh),
        out_shape=pltpu.VMEM((local_rows * nh, GROUP * HD), BF16),
        in_specs=[any_spec] * 6,
        out_specs=vmem_spec,
        scratch_shapes=[
            pltpu.VMEM(queries.shape, BF16),
            pltpu.VMEM(stretch_keys.shape, BF16),
            pltpu.VMEM(stretch_values.shape, BF16),
            pltpu.SMEM(cache_lengths.shape, jnp.int32),
            pltpu.VMEM(cache_keys.shape, BF16),
            pltpu.VMEM(cache_values.shape, BF16),
            pltpu.VMEM((n, msg_rows, HD), BF16),
            pltpu.VMEM((2, nh, local_rows, HD), BF16),
            pltpu.VMEM((2, NEAR, HD), F32),
            pltpu.VMEM((nz, owner_rows, HD), BF16),
            pltpu.VMEM((nz, 2, 128), F32),
            pltpu.VMEM((nz, owner_rows, HD), BF16),
            pltpu.VMEM((nz, 2, 128), F32),
            dma((4,)),
            dma((2 * REQS,)),
            dma,
            dma((n // BLOCK_SRC,)),
            dma,
            dma,
            dma,
            dma,
            dma,
            dma,
        ],
        compiler_params=pltpu.CompilerParams(
            collective_id=0, has_side_effects=True, vmem_limit_bytes=63 * 1024 * 1024
        ),
    )(queries, cache_keys, cache_values, stretch_keys, stretch_values, cache_lengths)


def solution(mesh):
    in_specs = (
        P(("groups", "grid", "head"), None),
        P("groups", "grid", "head"),
        P("groups", "grid", "head"),
        P(("groups", "grid", "head"), None),
        P(("groups", "grid", "head"), None),
        P("groups"),
    )
    out_specs = P(("groups", "grid"), "head")
    return jax.shard_map(shards, mesh=mesh, in_specs=in_specs, out_specs=out_specs, check_vma=False)
```
